256 devices in a mesh: outer: 16 (over z_lo, y, core), inner: 4 (over z_hi), dp: 4 (over x).
Axes of the slice: x: 4, y: 4, z: 8 (z_hi: 4, z_lo: 2; z = z_hi * 2 + z_lo), core: 2. Of those that a mesh axis runs over, the one named last changes fastest.
Arguments:
- queries: bfloat16 [4, 8192, 2048], P('dp', ('outer', 'inner')), may hold values from -9 to 9
- keys: bfloat16 [4, 8192, 2048], P('dp', ('outer', 'inner')), may hold values from -9 to 9
- values: bfloat16 [4, 8192, 2048], P('dp', ('outer', 'inner')), may hold values from -6 to 6
- out_grad: bfloat16 [4, 8192, 2048], P('dp', ('outer', 'inner')), may hold values from -15 to 15
- gain: float32 [2048], replicated, may hold values from 0.1 to 1.9
- block_order: int32 [128], P(('outer', 'inner')), may hold values from 0 to 127, each once
- start: int32 [1], replicated, may hold values from 1 to 3
Outputs:
- attended: bfloat16 [4, 8192, 2048], P('dp', ('outer', 'inner'))
- query_grad: bfloat16 [4, 8192, 2048], P('dp', ('outer', 'inner'))
- key_grad: bfloat16 [4, 8192, 2048], P('dp', ('outer', 'inner'))
- value_grad: bfloat16 [4, 8192, 2048], P('dp', ('outer', 'inner'))
- gain_grad: float32 [2048], replicated
The draws below stay inside these ranges and needn't reach their ends.
Inputs may be any that keep to these rules, and one draw needn't show every extreme that they name: `block_order`: a permutation of the block numbers.
All inputs are finite; a program needn't handle non-finite values.
Results may differ from the reference program's by a relative error of at most 0.025.
Values may be sent and summed in bfloat16 or wider, within the bound.
No kernel may reach another device: no remote copies, remote signals or barrier semaphores. Data moves between devices by JAX's collectives and lax.ppermute only.
A program may use at most 128 MiB of HBM per device.

```python
import math
import jax
import jax.numpy as jnp
from jax import lax

HEADS = 16
HEAD_DIM = 128
TOK_DEV = 128
SEQS = 4
SEQ = 8192
BLOCKS = 128
N_OUTER = 16
N_INNER = 4


def draw_queries(key, part):
    key = jax.random.fold_in(key, 3)
    shape_all = (SEQS, SEQ, HEADS * HEAD_DIM)
    drawn = jnp.clip(1.3 * jax.random.normal(key, shape_all), -8.0, 8.0)
    return drawn.astype(jnp.bfloat16)


def draw_keys(key, part):
    key = jax.random.fold_in(key, 5)
    shape_all = (SEQS, SEQ, HEADS * HEAD_DIM)
    drawn = jnp.clip(1.3 * jax.random.normal(key, shape_all), -8.0, 8.0)
    return drawn.astype(jnp.bfloat16)


def levels(key, extent, split, smallest, top_value):
    factor_of = 1.0
    for dim, blocks in split:
        steps = jax.random.uniform(jax.random.fold_in(jax.random.fold_in(key, 6), dim), (blocks,), jnp.float32, smallest / len(split), top_value / len(split))
        factor_of = factor_of * jnp.repeat(jnp.exp(steps), extent[dim] // blocks).reshape((-1,) + (1,) * (len(extent) - 1 - dim))
    return factor_of


def centred(key, shape, deviation, most, shards=(), held_as=jnp.bfloat16):
    loudness = levels(key, shape, shards, -0.22, 0.18) if shards else 1.0
    array = jax.random.normal(key, shape, jnp.float32) * deviation * loudness
    return jnp.minimum(jnp.maximum(array, -most), most).astype(held_as)


def setup_inputs(seed: int = 0) -> dict:
    streams_of = jax.random.split(jax.random.key(seed), 8)
    return {
        "queries": draw_queries(jax.random.fold_in(streams_of[7], 71), 0),
        "keys": draw_keys(jax.random.fold_in(streams_of[7], 71), 0),
        "values": centred(streams_of[2], (SEQS, SEQ, HEADS * HEAD_DIM), 1.0, 6.0, ((0, 4), (1, 64))),
        "out_grad": centred(streams_of[3], (SEQS, SEQ, HEADS * HEAD_DIM), 2.5, 15.0, ((0, 4), (1, 64))),
        "gain": jnp.clip(1.0 + 0.18 * jax.random.normal(streams_of[4], (HEADS * HEAD_DIM,), jnp.float32), 0.1, 1.9),
        "block_order": jax.random.permutation(streams_of[5], BLOCKS).astype(jnp.int32),
        "start": jax.random.randint(streams_of[6], (1,), 1, N_INNER).astype(jnp.int32),
    }


def attend(query_part, key_part, value_part, grad_part, query_positions, key_positions):
    local_rows, channels = query_part.shape
    key_count = key_part.shape[0]
    span = 4 * HEAD_DIM
    score_scale = HEAD_DIM ** (-0.5)
    visible = key_positions[None, :] <= query_positions[:, None]
    outputs = []
    query_grads = []
    key_grads = []
    value_grads = []
    for column_start in range(0, channels, span):
        query_heads = query_part[:, column_start:column_start + span].reshape(local_rows, 4, HEAD_DIM).astype(jnp.float32)
        key_heads = key_part[:, column_start:column_start + span].reshape(key_count, 4, HEAD_DIM).astype(jnp.float32)
        value_heads = value_part[:, column_start:column_start + span].reshape(key_count, 4, HEAD_DIM).astype(jnp.float32)
        grad_heads = grad_part[:, column_start:column_start + span].reshape(local_rows, 4, HEAD_DIM).astype(jnp.float32)
        scores = jnp.einsum('qhd,khd->hqk', query_heads, key_heads) * score_scale
        scores = jnp.where(visible[None], scores, -jnp.inf)
        row_max = lax.optimization_barrier(jnp.max(scores, axis=-1, keepdims=True))
        exp_scores = jnp.exp(scores - row_max)
        weights = exp_scores / lax.optimization_barrier(jnp.sum(exp_scores, axis=-1, keepdims=True))
        weights_bf = weights.astype(jnp.bfloat16)
        attended_part = jnp.einsum('hqk,khd->qhd', weights_bf.astype(jnp.float32), value_heads).astype(jnp.bfloat16)
        row_dot = lax.optimization_barrier(jnp.sum(grad_heads * attended_part.astype(jnp.float32), axis=-1))
        prob_grad = jnp.einsum('qhd,khd->hqk', grad_heads, value_heads)
        score_grad = (weights * (prob_grad - row_dot.T[:, :, None])).astype(jnp.bfloat16)
        query_grad_part = (jnp.einsum('hqk,khd->qhd', score_grad.astype(jnp.float32), key_heads) * score_scale).astype(jnp.bfloat16)
        key_grad_part = jnp.einsum('hqk,qhd->khd', score_grad.astype(jnp.float32), query_heads) * score_scale
        value_grad_part = jnp.einsum('hqk,qhd->khd', weights_bf.astype(jnp.float32), grad_heads)
        outputs.append(attended_part.reshape(local_rows, span))
        query_grads.append(query_grad_part.reshape(local_rows, span))
        key_grads.append(key_grad_part.reshape(key_count, span))
        value_grads.append(value_grad_part.reshape(key_count, span))
    return (jnp.concatenate(outputs, axis=1), jnp.concatenate(query_grads, axis=1), jnp.concatenate(key_grads, axis=1), jnp.concatenate(value_grads, axis=1))

def reference(queries, keys, values, out_grad, gain, block_order, start):
    half_rows = TOK_DEV // 2
    shard_count = N_OUTER * N_INNER
    channels = HEADS * HEAD_DIM
    positions = (block_order[:, None] * half_rows + jnp.arange(half_rows, dtype=jnp.int32)[None, :]).reshape(shard_count, TOK_DEV)
    step_offset = start[0]
    keyed_all = (keys.astype(jnp.float32) * gain).astype(jnp.bfloat16)
    attended_list = []
    query_list = []
    key_list = []
    value_list = []
    gain_sum = jnp.zeros((channels,), jnp.float32)
    for sequence in range(SEQS):
        keyed_seq = keyed_all[sequence].reshape(shard_count, TOK_DEV, channels)
        value_seq = values[sequence].reshape(shard_count, TOK_DEV, channels)
        query_seq = queries[sequence].reshape(shard_count, TOK_DEV, channels)
        grad_seq = out_grad[sequence].reshape(shard_count, TOK_DEV, channels)

        def visit_device(totals, device):
            outer_pos = device // N_INNER
            inner_pos = device % N_INNER
            prior_rows = (outer_pos - 1) % N_OUTER * N_INNER + jnp.arange(N_INNER, dtype=jnp.int32)
            step_source = outer_pos * N_INNER + (inner_pos - step_offset) % N_INNER
            sources = jnp.concatenate([device[None], step_source[None], prior_rows]).astype(jnp.int32)
            key_rows = keyed_seq[sources].reshape(-1, channels)
            value_rows = value_seq[sources].reshape(-1, channels)
            attended_part, query_grad_part, key_part, value_part = attend(query_seq[device], key_rows, value_rows, grad_seq[device], positions[device], positions[sources].reshape(-1))
            key_round = lax.optimization_barrier(key_part.astype(jnp.bfloat16)).astype(jnp.float32)
            value_round = lax.optimization_barrier(value_part.astype(jnp.bfloat16)).astype(jnp.float32)
            total_keys, total_values = totals
            total_keys = total_keys.at[sources].add(key_round.reshape(-1, TOK_DEV, channels))
            total_values = total_values.at[sources].add(value_round.reshape(-1, TOK_DEV, channels))
            return ((total_keys, total_values), (attended_part, query_grad_part))
        empty = jnp.zeros((shard_count, TOK_DEV, channels), jnp.float32)
        (total_keys, total_values), (attended_seq, query_grad_seq) = lax.scan(visit_device, (empty, empty), jnp.arange(shard_count, dtype=jnp.int32))
        total_keys = total_keys.reshape(SEQ, channels)
        total_values = total_values.reshape(SEQ, channels)
        attended_list.append(attended_seq.reshape(SEQ, channels))
        query_list.append(query_grad_seq.reshape(SEQ, channels))
        key_list.append((total_keys * gain).astype(jnp.bfloat16))
        value_list.append(total_values.astype(jnp.bfloat16))
        gain_sum = gain_sum + lax.optimization_barrier(jnp.sum(total_keys * keys[sequence].astype(jnp.float32), axis=0))
    gain_grad = gain_sum / math.sqrt(SEQS * SEQ)
    return (jnp.stack(attended_list), jnp.stack(query_list), jnp.stack(key_list), jnp.stack(value_list), gain_grad)
```

```python
import functools
import math

import jax
import jax.numpy as jnp
from jax import lax
from jax.experimental import pallas as pl
from jax.experimental.pallas import tpu as pltpu
from jax.sharding import PartitionSpec as P

HEAD_DIM = 128
ROWS = 128
SHARDS = 4
ORDER_ROWS = 16
CHUNKS = 2
F32 = jnp.float32
BF16 = jnp.bfloat16


def permuted(value, axis, steps):
    count = lax.axis_size(axis)
    pairs = [(source, (source + steps) % count) for source in range(count)]
    return lax.ppermute(value, axis, pairs)


def vmem_spec():
    return pl.BlockSpec(memory_space=pltpu.VMEM)


def smem_spec():
    return pl.BlockSpec(memory_space=pltpu.SMEM)


def pack_kv_kernel(width, place, keys, values, *outs):
    rows = lax.broadcasted_iota(jnp.int32, (ORDER_ROWS, width), 0)
    numbers = jnp.where(rows < ORDER_ROWS // 2, place[1], place[2]).astype(F32).astype(BF16)
    for k, out in enumerate(outs):
        column = pl.multiple_of(lax.rem(place[0] + k, SHARDS) * width, width)
        out[0:ROWS] = keys[0, :, pl.ds(column, width)]
        out[ROWS : 2 * ROWS] = values[0, :, pl.ds(column, width)]
        out[2 * ROWS :] = numbers


def pack_kv(place, keys, values):
    width = keys.shape[2] // SHARDS
    out = jax.ShapeDtypeStruct((2 * ROWS + ORDER_ROWS, width), BF16)
    return pl.pallas_call(
        functools.partial(pack_kv_kernel, width),
        out_shape=(out,) * SHARDS,
        in_specs=[smem_spec(), vmem_spec(), vmem_spec()],
        out_specs=(vmem_spec(),) * SHARDS,
        name="pack_kv",
    )(place, keys, values)


def pack_qd_kernel(width, scalars, queries, grads, *outs):
    part = width // CHUNKS
    for c in range(CHUNKS):
        for k in range(SHARDS):
            start = lax.rem(scalars[0] + k, SHARDS) * width + c * part
            column = pl.multiple_of(start, part)
            out = outs[c * SHARDS + k]
            out[0:ROWS] = queries[0, :, pl.ds(column, part)]
            out[ROWS:] = grads[0, :, pl.ds(column, part)]


def pack_qd(scalars, queries, grads):
    width = queries.shape[2] // SHARDS
    out = jax.ShapeDtypeStruct((2 * ROWS, width // CHUNKS), BF16)
    return pl.pallas_call(
        functools.partial(pack_qd_kernel, width),
        out_shape=(out,) * (CHUNKS * SHARDS),
        in_specs=[smem_spec(), vmem_spec(), vmem_spec()],
        out_specs=(vmem_spec(),) * (CHUNKS * SHARDS),
        name="pack_qd",
    )(scalars, queries, grads)


def unpack_kernel(width, scalars, *refs):
    count = CHUNKS * SHARDS
    parts, outs = refs[:count], refs[count:]
    part = width // CHUNKS
    for c in range(CHUNKS):
        for k in range(SHARDS):
            start = lax.rem(scalars[0] + k, SHARDS) * width + c * part
            column = pl.multiple_of(start, part)
            for n, out in enumerate(outs):
                rows = parts[c * SHARDS + k][n * ROWS : (n + 1) * ROWS]
                out[0, :, pl.ds(column, part)] = rows


def unpack(scalars, parts, name):
    part = parts[0].shape[1]
    out = jax.ShapeDtypeStruct((1, ROWS, part * CHUNKS * SHARDS), BF16)
    return pl.pallas_call(
        functools.partial(unpack_kernel, part * CHUNKS),
        out_shape=(out, out),
        in_specs=[smem_spec()] + [vmem_spec()] * len(parts),
        out_specs=(vmem_spec(), vmem_spec()),
        name=name,
    )(scalars, *parts)


def dot_nn(a, b):
    return lax.dot_general(a, b, (((1,), (0,)), ((), ())), preferred_element_type=F32)


def dot_nt(a, b):
    return lax.dot_general(a, b, (((1,), (1,)), ((), ())), preferred_element_type=F32)


def attend_kernel(scalars, *refs):
    own_kv, prior_kv, qd = refs[0:4], refs[4:8], refs[8:12]
    gain = refs[12]
    ad_out = refs[13:17]
    own_out, prior_out, gain_out = refs[17:20]
    own, own_t, prior, prior_t, kpos, qpos, q_all, s_all, w_self, w_step, w_prior = refs[20:]
    start = scalars[1]
    group = SHARDS * ROWS
    score_scale = HEAD_DIM ** (-0.5)
    exponent_scale = score_scale * math.log2(math.e)
    half = ROWS // 2
    key_at, value_at = 0, 1
    query_at, grad_at = 0, 1
    weight_at, score_at = 0, 1

    @pl.when(pl.program_id(0) == 0)
    def _():
        lane = lax.broadcasted_iota(jnp.int32, (1, ROWS), 1)
        lanes = jnp.where(lane < half, lane, lane - half).astype(F32)
        row = lax.broadcasted_iota(jnp.int32, (half, ROWS), 0).astype(F32)
        for s, ref in enumerate(tuple(own_kv) + tuple(prior_kv)):
            numbers = ref[2 * ROWS : 2 * ROWS + ORDER_ROWS].astype(F32)
            first = numbers[0:1] * half
            second = numbers[ORDER_ROWS // 2 : ORDER_ROWS // 2 + 1] * half
            kpos[s, 0:half] = row + first
            kpos[s, half:ROWS] = row + second
            if s < SHARDS:
                qpos[s : s + 1] = jnp.where(lane < half, first, second) + lanes

    gain_row = gain[...]
    for s in range(SHARDS):
        rows = slice(s * ROWS, (s + 1) * ROWS)
        for n in (key_at, value_at):
            part = own_kv[s][n * ROWS : (n + 1) * ROWS]
            if n == key_at:
                part = (part.astype(F32) * gain_row).astype(BF16)
            own[n, s] = part
            own_t[n, s] = part.T
            part = prior_kv[s][n * ROWS : (n + 1) * ROWS]
            if n == key_at:
                part = (part.astype(F32) * gain_row).astype(BF16)
            prior[n, rows] = part
            prior_t[n, :, rows] = part.T
        q_all[query_at, s] = qd[s][0:ROWS]
        q_all[grad_at, s] = qd[s][ROWS : 2 * ROWS]
    for n in (0, 1):
        s_all[n] = dot_nt(prior[n], q_all[n].reshape(group, HEAD_DIM))

    for a in range(SHARDS):
        step = lax.rem(start + a, SHARDS)
        cols = slice(a * ROWS, (a + 1) * ROWS)
        query, grad = q_all[query_at, a], q_all[grad_at, a]

        def masked(raw, positions):
            return jnp.where(positions <= qpos[a : a + 1], raw * exponent_scale, -jnp.inf)

        scores = jnp.concatenate(
            [
                masked(dot_nt(own[key_at, a], query), kpos[a]),
                masked(dot_nt(own[key_at, step], query), kpos[step]),
                masked(s_all[0, :, cols], kpos[SHARDS:].reshape(group, ROWS)),
            ],
            axis=0,
        )
        exps = jnp.exp2(scores - jnp.max(scores, axis=0, keepdims=True))
        weights = exps * (1.0 / jnp.sum(exps, axis=0, keepdims=True))
        weights_bf = weights.astype(BF16)
        w_self[weight_at, a] = weights_bf[0:ROWS]
        w_step[weight_at, a] = weights_bf[ROWS : 2 * ROWS]
        w_prior[weight_at, :, cols] = weights_bf[2 * ROWS :]
        attended_t = (
            dot_nn(prior_t[value_at], weights_bf[2 * ROWS :])
            + dot_nn(own_t[value_at, a], weights_bf[0:ROWS])
            + dot_nn(own_t[value_at, step], weights_bf[ROWS : 2 * ROWS])
        )
        ad_out[a][0:ROWS] = attended_t.T.astype(BF16)
        rounded = attended_t.astype(BF16).astype(F32)
        row_dot = jnp.sum(grad.astype(F32).T * rounded, axis=0, keepdims=True)
        weight_grad = jnp.concatenate(
            [
                dot_nt(own[value_at, a], grad),
                dot_nt(own[value_at, step], grad),
                s_all[1, :, cols],
            ],
            axis=0,
        )
        score_grad = (weights * (weight_grad - row_dot)).astype(BF16)
        w_self[score_at, a] = score_grad[0:ROWS]
        w_step[score_at, a] = score_grad[ROWS : 2 * ROWS]
        w_prior[score_at, :, cols] = score_grad[2 * ROWS :]
        query_grad_t = (
            dot_nn(prior_t[key_at], score_grad[2 * ROWS :])
            + dot_nn(own_t[key_at, a], score_grad[0:ROWS])
            + dot_nn(own_t[key_at, step], score_grad[ROWS : 2 * ROWS])
        )
        ad_out[a][ROWS : 2 * ROWS] = (query_grad_t * score_scale).T.astype(BF16)

    gain_sum = jnp.zeros((1, HEAD_DIM), F32)
    queries, grads = (q_all[n].reshape(group, HEAD_DIM) for n in (0, 1))
    prior_key = dot_nn(w_prior[score_at], queries) * score_scale
    prior_value = dot_nn(w_prior[weight_at], grads)
    for s in range(SHARDS):
        key_part = prior_key[s * ROWS : (s + 1) * ROWS]
        prior_out[2 * s * ROWS : (2 * s + 1) * ROWS] = key_part.astype(BF16)
        value_part = prior_value[s * ROWS : (s + 1) * ROWS]
        prior_out[(2 * s + 1) * ROWS : (2 * s + 2) * ROWS] = value_part.astype(BF16)
        raw = prior_kv[s][0:ROWS].astype(F32)
        gain_sum += jnp.sum(key_part * raw, axis=0, keepdims=True)
    for s in range(SHARDS):
        other = lax.rem(s + SHARDS - start, SHARDS)
        key_part = (
            dot_nn(w_self[score_at, s], q_all[query_at, s])
            + dot_nn(w_step[score_at, other], q_all[query_at, other])
        ) * score_scale
        value_part = dot_nn(w_self[weight_at, s], q_all[grad_at, s]) + dot_nn(
            w_step[weight_at, other], q_all[grad_at, other]
        )
        own_out[2 * s * ROWS : (2 * s + 1) * ROWS] = key_part
        own_out[(2 * s + 1) * ROWS : (2 * s + 2) * ROWS] = value_part
        raw = own_kv[s][0:ROWS].astype(F32)
        gain_sum += jnp.sum(key_part * raw, axis=0, keepdims=True)
    gain_out[...] = gain_sum


def attend(scalars, chunk, own_kv, prior_kv, qd, gain_row):
    part = qd[0].shape[1]
    heads = part // HEAD_DIM
    first = chunk * heads
    per_device = CHUNKS * heads
    kv_rows = 2 * ROWS + ORDER_ROWS
    group = SHARDS * ROWS
    kv_spec = pl.BlockSpec((kv_rows, HEAD_DIM), lambda h, sc: (0, first + h))
    qd_spec = pl.BlockSpec((2 * ROWS, HEAD_DIM), lambda h, sc: (0, h))
    gain_spec = pl.BlockSpec((1, HEAD_DIM), lambda h, sc: (0, sc[0] * per_device + first + h))
    wide_spec = pl.BlockSpec((2 * group, HEAD_DIM), lambda h, sc: (0, h))
    row_spec = pl.BlockSpec((1, HEAD_DIM), lambda h, sc: (0, h))
    return pl.pallas_call(
        attend_kernel,
        grid_spec=pltpu.PrefetchScalarGridSpec(
            num_scalar_prefetch=1,
            grid=(heads,),
            in_specs=[kv_spec] * 8 + [qd_spec] * 4 + [gain_spec],
            out_specs=[qd_spec] * 4 + [wide_spec, wide_spec, row_spec],
            scratch_shapes=[
                pltpu.VMEM((2, SHARDS, ROWS, HEAD_DIM), BF16),
                pltpu.VMEM((2, SHARDS, HEAD_DIM, ROWS), BF16),
                pltpu.VMEM((2, group, HEAD_DIM), BF16),
                pltpu.VMEM((2, HEAD_DIM, group), BF16),
                pltpu.VMEM((2 * SHARDS, ROWS, ROWS), F32),
                pltpu.VMEM((8, ROWS), F32),
                pltpu.VMEM((2, SHARDS, ROWS, HEAD_DIM), BF16),
                pltpu.VMEM((2, group, group), F32),
                pltpu.VMEM((2, SHARDS, ROWS, ROWS), BF16),
                pltpu.VMEM((2, SHARDS, ROWS, ROWS), BF16),
                pltpu.VMEM((2, group, group), BF16),
            ],
        ),
        out_shape=(jax.ShapeDtypeStruct((2 * ROWS, part), BF16),) * 4
        + (
            jax.ShapeDtypeStruct((2 * group, part), F32),
            jax.ShapeDtypeStruct((2 * group, part), BF16),
            jax.ShapeDtypeStruct((1, part), F32),
        ),
        compiler_params=pltpu.CompilerParams(
            dimension_semantics=("arbitrary",), vmem_limit_bytes=32 * 1024 * 1024
        ),
        cost_estimate=pl.CostEstimate(
            flops=heads * 12 * group * (group + 2 * ROWS) * HEAD_DIM,
            bytes_accessed=heads * 14 * group * HEAD_DIM * 2,
            transcendentals=heads * group * (group + 2 * ROWS),
        ),
        name="attend",
    )(scalars, *own_kv, *prior_kv, *qd, gain_row)


def finish_kernel(scalars, own, back, gain, *outs):
    gain_row = gain[...]
    for s in range(SHARDS):
        rows = pl.ds(2 * s * ROWS, ROWS)
        total = own[rows] + back[rows].astype(F32)
        outs[s][0:ROWS] = (total * gain_row).astype(BF16)
        rows = pl.ds((2 * s + 1) * ROWS, ROWS)
        outs[s][ROWS : 2 * ROWS] = (own[rows] + back[rows].astype(F32)).astype(BF16)


def finish(scalars, chunk, own, back, gain_row):
    part = own.shape[1]
    heads = part // HEAD_DIM
    width = 2 * HEAD_DIM if heads % 2 == 0 else HEAD_DIM
    steps = part // width
    group = SHARDS * ROWS
    wide_spec = pl.BlockSpec((2 * group, width), lambda h, sc: (0, h))
    gain_spec = pl.BlockSpec((1, width), lambda h, sc: (0, (sc[0] * CHUNKS + chunk) * steps + h))
    out_spec = pl.BlockSpec((2 * ROWS, width), lambda h, sc: (0, h))
    return pl.pallas_call(
        finish_kernel,
        grid_spec=pltpu.PrefetchScalarGridSpec(
            num_scalar_prefetch=1,
            grid=(steps,),
            in_specs=[wide_spec, wide_spec, gain_spec],
            out_specs=[out_spec] * SHARDS,
        ),
        out_shape=(jax.ShapeDtypeStruct((2 * ROWS, part), BF16),) * SHARDS,
        compiler_params=pltpu.CompilerParams(
            dimension_semantics=("arbitrary",), vmem_limit_bytes=32 * 1024 * 1024
        ),
        cost_estimate=pl.CostEstimate(
            flops=4 * group * part, bytes_accessed=16 * group * part, transcendentals=0
        ),
        name="finish",
    )(scalars, own, back, gain_row)


def sum_of_four(value, axis, stride):
    return value + (
        permuted(value, axis, stride)
        + permuted(value, axis, 2 * stride)
        + permuted(value, axis, 3 * stride)
    )


def body(queries, keys, values, out_grad, gain, block_order, start):
    inner = lax.axis_index("inner").astype(jnp.int32)
    place = jnp.stack([inner, block_order[0], block_order[1]])
    scalars = jnp.stack([inner, start[0]])
    gain_row = gain[None]

    kv = pack_kv(place, keys, values)
    own_kv = [kv[0]] + [permuted(kv[k], "inner", k) for k in range(1, SHARDS)]
    packed = pack_qd(scalars, queries, out_grad)
    prior_kv = [permuted(part, "outer", 1) for part in own_kv]
    ad_parts, dkv_parts, gain_terms = [], [], []
    for c in range(CHUNKS):
        mine = packed[c * SHARDS : (c + 1) * SHARDS]
        qd = [mine[0]] + [permuted(mine[k], "inner", k) for k in range(1, SHARDS)]
        results = attend(scalars, c, own_kv, prior_kv, qd, gain_row)
        ad, (own, prior, gain_term) = results[:SHARDS], results[SHARDS:]
        gain_terms.append(gain_term)
        ad_parts += [ad[0]] + [permuted(ad[k], "inner", -k) for k in range(1, SHARDS)]
        back = permuted(prior, "outer", -1)
        dkv = finish(scalars, c, own, back, gain_row)
        dkv_parts += [dkv[0]] + [permuted(dkv[k], "inner", -k) for k in range(1, SHARDS)]
    attended, query_grad = unpack(scalars, ad_parts, "unpack_ad")
    key_grad, value_grad = unpack(scalars, dkv_parts, "unpack_dkv")

    term = jnp.concatenate(gain_terms, axis=1)
    term = sum_of_four(term, "dp", 1)
    term = sum_of_four(term, "outer", 4)
    term = sum_of_four(term, "outer", 1)
    terms = jnp.concatenate([term] + [permuted(term, "inner", -k) for k in range(1, SHARDS)])
    terms = jnp.roll(terms, inner, axis=0)
    token_count = (
        ROWS * lax.axis_size("inner") * lax.axis_size("outer") * lax.axis_size("dp")
    )
    gain_grad = terms.reshape(-1) / math.sqrt(token_count)
    return attended, query_grad, key_grad, value_grad, gain_grad


def solution(mesh):
    rows = P("dp", ("outer", "inner"), None)
    in_specs = (rows, rows, rows, rows, P(), P(("outer", "inner")), P())
    out_specs = (rows, rows, rows, rows, P())
    return jax.shard_map(body, mesh=mesh, in_specs=in_specs, out_specs=out_specs, check_vma=False)
```

```python
import functools
import math

import jax
import jax.numpy as jnp
from jax import lax
from jax.experimental import pallas as pl
from jax.experimental.pallas import tpu as pltpu
from jax.sharding import PartitionSpec as P

HEAD_DIM = 128
ROWS = 128
SHARDS = 4
EXTRA_ROWS = 16
KV_ROWS = 2 * ROWS + EXTRA_ROWS
VMEM_BYTES = 56 * 1024 * 1024
F32 = jnp.float32
BF16 = jnp.bfloat16


def permuted(value, axis, steps):
    count = lax.axis_size(axis)
    pairs = [(source, (source + steps) % count) for source in range(count)]
    return lax.ppermute(value, axis, pairs)


def vmem_spec():
    return pl.BlockSpec(memory_space=pltpu.VMEM)


def smem_spec():
    return pl.BlockSpec(memory_space=pltpu.SMEM)


def any_spec():
    return pl.BlockSpec(memory_space=pl.ANY)


def place_columns(k, width):
    return block_columns(lax.rem(lax.axis_index("inner") + k, SHARDS), width)


def block_columns(place, width):
    half = width // 2
    turn = lax.axis_index("outer") // (lax.axis_size("outer") // 2)
    first = place * width
    second = lax.rem(place + turn, SHARDS) * width + half
    return (
        (pl.ds(pl.multiple_of(first, half), half), slice(0, half)),
        (pl.ds(pl.multiple_of(second, half), half), slice(half, width)),
    )


def put_kv(out, k, order, keys, values):
    width = out.shape[1]
    for columns, here in place_columns(k, width):
        out[0:ROWS, here] = keys[0, :, columns]
        out[ROWS : 2 * ROWS, here] = values[0, :, columns]
    rows = lax.broadcasted_iota(jnp.int32, (EXTRA_ROWS, width), 0)
    numbers = jnp.where(rows < EXTRA_ROWS // 2, order[0], order[1])
    out[2 * ROWS : KV_ROWS] = numbers.astype(F32).astype(BF16)


def put_qd(out, first, k, queries, grads):
    for columns, here in place_columns(k, out.shape[1]):
        out[first : first + ROWS, here] = queries[0, :, columns]
        out[first + ROWS : first + 2 * ROWS, here] = grads[0, :, columns]


def join_kernel(*refs):
    parts, outs = refs[:-2], refs[-2:]
    half = parts[0].shape[1] // 2
    for n, out in enumerate(outs):
        for s, part in enumerate(parts):
            rows = slice(s * KV_ROWS, (s + 1) * KV_ROWS)
            out[rows] = part[0:KV_ROWS, n * half : (n + 1) * half]


def join(parts):
    out = jax.ShapeDtypeStruct((len(parts) * KV_ROWS, parts[0].shape[1] // 2), BF16)
    return pl.pallas_call(
        join_kernel,
        out_shape=(out, out),
        in_specs=[vmem_spec()] * len(parts),
        out_specs=(vmem_spec(),) * 2,
        compiler_params=pltpu.CompilerParams(vmem_limit_bytes=VMEM_BYTES),
        name="join",
    )(*parts)


def pack_kernel(order, queries, keys, values, grads, *outs):
    for k, out in enumerate(outs):
        put_kv(out, k, order, keys, values)
        put_qd(out, KV_ROWS, k, queries, grads)


def pack(order, queries, keys, values, grads):
    out = jax.ShapeDtypeStruct((KV_ROWS + 2 * ROWS, keys.shape[2] // SHARDS), BF16)
    return pl.pallas_call(
        pack_kernel,
        out_shape=(out,) * SHARDS,
        in_specs=[smem_spec()] + [vmem_spec()] * 4,
        out_specs=(vmem_spec(),) * SHARDS,
        compiler_params=pltpu.CompilerParams(vmem_limit_bytes=VMEM_BYTES),
        name="pack",
    )(order, queries, keys, values, grads)


def copies_out(k, part, first, outs, sems):
    copies = []
    for h, (columns, here) in enumerate(place_columns(k, part.shape[1])):
        for n, out in enumerate(outs):
            source = part.at[first + n * ROWS : first + (n + 1) * ROWS, here]
            sem = sems.at[2 * h + n]
            copies.append(pltpu.make_async_copy(source, out.at[0, :, columns], sem))
    return copies


def unpack_early_kernel(part_0, part_1, part_3, attended, query_grad, sems):
    outs = (attended, query_grad)
    copies = copies_out(0, part_0, 0, outs, sems.at[0])
    copies += copies_out(1, part_1, 0, outs, sems.at[1])
    copies += copies_out(3, part_3, 0, outs, sems.at[2])
    for copy in copies:
        copy.start()
    for copy in copies:
        copy.wait()


def unpack_early(parts):
    out = jax.ShapeDtypeStruct((1, ROWS, parts[0].shape[1] * SHARDS), BF16)
    return pl.pallas_call(
        unpack_early_kernel,
        out_shape=(out, out),
        in_specs=[vmem_spec()] * 3,
        out_specs=(any_spec(), any_spec()),
        scratch_shapes=[pltpu.SemaphoreType.DMA((3, 4))],
        compiler_params=pltpu.CompilerParams(vmem_limit_bytes=VMEM_BYTES),
        name="unpack_early",
    )(*parts)


def unpack_kernel(gain_scale, *refs):
    parts, terms = refs[:SHARDS], refs[SHARDS]
    attended, query_grad, key_grad, value_grad, gain_grad, sems = refs[SHARDS + 3 :]
    copies = []
    for k, part in enumerate(parts):
        copies += copies_out(k, part, 0, (key_grad, value_grad), sems.at[k])
    copies += copies_out(2, parts[2], 2 * ROWS, (attended, query_grad), sems.at[SHARDS])
    for copy in copies:
        copy.start()
    for n in range(SHARDS):
        for columns, here in block_columns(lax.axis_index("inner") ^ n, terms.shape[1]):
            gain_grad[:, columns] = terms[n : n + 1, here] * gain_scale
    for copy in copies:
        copy.wait()


def unpack(parts, terms, attended, query_grad, gain_scale):
    out = jax.ShapeDtypeStruct(attended.shape, BF16)
    count = SHARDS + 1
    return pl.pallas_call(
        functools.partial(unpack_kernel, gain_scale),
        out_shape=(out,) * 4 + (jax.ShapeDtypeStruct((1, attended.shape[2]), F32),),
        in_specs=[vmem_spec()] * count + [any_spec()] * 2,
        out_specs=(any_spec(),) * 4 + (vmem_spec(),),
        scratch_shapes=[pltpu.SemaphoreType.DMA((SHARDS + 1, 4))],
        input_output_aliases={count: 0, count + 1: 1},
        compiler_params=pltpu.CompilerParams(vmem_limit_bytes=VMEM_BYTES),
        name="unpack",
    )(*parts, terms, attended, query_grad)


def dot_nn(a, b):
    return lax.dot_general(a, b, (((1,), (0,)), ((), ())), preferred_element_type=F32)


def dot_nt(a, b):
    return lax.dot_general(a, b, (((1,), (1,)), ((), ())), preferred_element_type=F32)


def attend_kernel(scalars, *refs):
    own_kv = refs[0:4]
    qd = [ref.at[KV_ROWS:] for ref in own_kv]
    halves = (refs[4:6], refs[6:8])
    prior_place = ((0, 0), (0, KV_ROWS), (1, 0), (0, 2 * KV_ROWS))
    gain = refs[8]
    ad_out = refs[9:13]
    own_out = refs[13]
    prior_outs, gain_out = refs[14:16], refs[16]
    own, own_t, prior, prior_t, raw_prior, kpos, qpos, q_all, s_all, w_all, step_part = refs[17:]
    head, heads = pl.program_id(0), pl.num_programs(0)
    start = scalars[1]
    group = SHARDS * ROWS
    score_scale = HEAD_DIM ** (-0.5)
    exponent_scale = score_scale * math.log2(math.e)
    half = ROWS // 2
    key_at, value_at = 0, 1
    query_at, grad_at = 0, 1
    weight_at, score_at = 0, 1

    in_first = head < heads // 2
    lane = lax.broadcasted_iota(jnp.int32, (1, ROWS), 1)
    lanes = jnp.where(lane < half, lane, lane - half).astype(F32)
    row = lax.broadcasted_iota(jnp.int32, (half, ROWS), 0).astype(F32)
    own_numbers = [ref[2 * ROWS : KV_ROWS] for ref in own_kv]
    prior_numbers = [
        jnp.where(in_first, *(parts[at][first + 2 * ROWS : first + KV_ROWS] for parts in halves))
        for at, first in prior_place
    ]
    for s, numbers in enumerate(own_numbers + prior_numbers):
        numbers = numbers.astype(F32)
        first = numbers[0:1] * half
        second = numbers[EXTRA_ROWS // 2 : EXTRA_ROWS // 2 + 1] * half
        kpos[s, 0:half] = row + first
        kpos[s, half:ROWS] = row + second
        if s < SHARDS:
            qpos[s : s + 1] = jnp.where(lane < half, first, second) + lanes

    gain_row = gain[...]
    for s in range(SHARDS):
        rows = slice(s * ROWS, (s + 1) * ROWS)
        for n in (key_at, value_at):
            part = own_kv[s][n * ROWS : (n + 1) * ROWS]
            if n == key_at:
                part = (part.astype(F32) * gain_row).astype(BF16)
            own[n, s] = part
            own_t[n, s] = part.T
        q_all[query_at, s] = qd[s][0:ROWS]
        q_all[grad_at, s] = qd[s][ROWS : 2 * ROWS]
    for s, (part_at, first) in enumerate(prior_place):
        rows = slice(s * ROWS, (s + 1) * ROWS)
        raw, value = (
            jnp.where(in_first, *(half[part_at][at : at + ROWS] for half in halves))
            for at in (first, first + ROWS)
        )
        raw_prior[rows] = raw
        key = (raw.astype(F32) * gain_row).astype(BF16)
        for n, part in ((key_at, key), (value_at, value)):
            prior[n, rows] = part
            prior_t[n, :, rows] = part.T

    steps = [lax.rem(start + a, SHARDS) for a in range(SHARDS)]
    columns = [slice(a * ROWS, (a + 1) * ROWS) for a in range(SHARDS)]
    for n in (0, 1):
        s_all[n, 2 * ROWS :] = dot_nt(prior[n], q_all[n].reshape(group, HEAD_DIM))
    for n in (0, 1):
        for a in range(SHARDS):
            s_all[n, 0:ROWS, columns[a]] = dot_nt(own[n, a], q_all[n, a])
            s_all[n, ROWS : 2 * ROWS, columns[a]] = dot_nt(own[n, steps[a]], q_all[n, a])

    for a in range(SHARDS):
        query_pos = qpos[a : a + 1]
        parts = []
        for first, positions in (
            (0, kpos[a]),
            (ROWS, kpos[steps[a]]),
            (2 * ROWS, kpos[SHARDS:].reshape(group, ROWS)),
        ):
            raw = s_all[0, first : first + positions.shape[0], columns[a]] * exponent_scale
            parts.append(jnp.where(positions <= query_pos, raw, -jnp.inf))
        scores = jnp.concatenate(parts, axis=0)
        exps = jnp.exp2(scores - jnp.max(scores, axis=0, keepdims=True))
        weights = exps * (1.0 / jnp.sum(exps, axis=0, keepdims=True))
        s_all[0, :, columns[a]] = weights
        w_all[weight_at, :, columns[a]] = weights.astype(BF16)

    def times_weights(n, which):
        total = dot_nn(prior_t[n], w_all[which, 2 * ROWS :])
        return [
            total[:, columns[a]]
            + dot_nn(own_t[n, a], w_all[which, 0:ROWS, columns[a]])
            + dot_nn(own_t[n, steps[a]], w_all[which, ROWS : 2 * ROWS, columns[a]])
            for a in range(SHARDS)
        ]

    attended_t = times_weights(value_at, weight_at)
    for a in range(SHARDS):
        ad_out[a][0:ROWS] = attended_t[a].T.astype(BF16)
        rounded = attended_t[a].astype(BF16).astype(F32)
        grad_t = q_all[grad_at, a].astype(F32).T
        row_dot = jnp.sum(grad_t * rounded, axis=0, keepdims=True)
        weights = s_all[0, :, columns[a]]
        score_grad = weights * (s_all[1, :, columns[a]] - row_dot)
        w_all[score_at, :, columns[a]] = score_grad.astype(BF16)
    query_grad_t = times_weights(key_at, score_at)
    for a in range(SHARDS):
        ad_out[a][ROWS : 2 * ROWS] = (query_grad_t[a] * score_scale).T.astype(BF16)

    gain_sum = jnp.zeros((1, HEAD_DIM), F32)
    queries, grads = (q_all[n].reshape(group, HEAD_DIM) for n in (0, 1))
    prior_key = dot_nn(w_all[score_at, 2 * ROWS :], queries) * score_scale
    prior_value = dot_nn(w_all[weight_at, 2 * ROWS :], grads)
    gain_sum += jnp.sum(prior_key * raw_prior[...].astype(F32), axis=0, keepdims=True)
    for half_at, out in enumerate(prior_outs):

        @pl.when(head // (heads // 2) == half_at)
        def _(out=out):
            for s in range(SHARDS):
                rows = slice(s * ROWS, (s + 1) * ROWS)
                out[2 * s * ROWS : (2 * s + 1) * ROWS] = prior_key[rows].astype(BF16)
                out[(2 * s + 1) * ROWS : (2 * s + 2) * ROWS] = prior_value[rows].astype(BF16)

    for n in (0, 1):
        which, source = ((score_at, query_at), (weight_at, grad_at))[n]
        for a in range(SHARDS):
            step_part[n, steps[a]] = dot_nn(w_all[which, ROWS : 2 * ROWS, columns[a]], q_all[source, a])
    for s in range(SHARDS):
        key_part = dot_nn(w_all[score_at, 0:ROWS, columns[s]], q_all[query_at, s])
        key_part = (key_part + step_part[0, s]) * score_scale
        value_part = dot_nn(w_all[weight_at, 0:ROWS, columns[s]], q_all[grad_at, s])
        value_part = value_part + step_part[1, s]
        own_out[2 * s * ROWS : (2 * s + 1) * ROWS] = key_part.astype(BF16)
        own_out[(2 * s + 1) * ROWS : (2 * s + 2) * ROWS] = value_part.astype(BF16)
        raw = own_kv[s][0:ROWS].astype(F32)
        gain_sum += jnp.sum(key_part * raw, axis=0, keepdims=True)
    gain_out[...] = jnp.broadcast_to(gain_sum, gain_out.shape)


def attend(scalars, own, prior_kv, gain_row):
    part = own[0].shape[1]
    heads = part // HEAD_DIM
    group = SHARDS * ROWS

    def column_spec(rows):
        return pl.BlockSpec((rows, HEAD_DIM), lambda h, sc: (0, h))

    half = heads // 2

    def half_spec(rows, n):
        if n == 0:
            return pl.BlockSpec((rows, HEAD_DIM), lambda h, sc: (0, jnp.minimum(h, half - 1)))
        return pl.BlockSpec((rows, HEAD_DIM), lambda h, sc: (0, jnp.maximum(h - half, 0)))

    gain_spec = pl.BlockSpec(
        (1, HEAD_DIM), lambda h, sc: (0, jnp.where(h < half, sc[0], sc[2]) * heads + h)
    )
    outs = [(2 * ROWS, part)] * 4 + [(2 * group, part)] + [(2 * group, part // 2)] * 2
    return pl.pallas_call(
        attend_kernel,
        grid_spec=pltpu.PrefetchScalarGridSpec(
            num_scalar_prefetch=1,
            grid=(heads,),
            in_specs=[column_spec(x.shape[0]) for x in own]
            + [half_spec(x.shape[0], n // 2) for n, x in enumerate(prior_kv)]
            + [gain_spec],
            out_specs=[column_spec(rows) for rows, _ in outs[:5]]
            + [half_spec(2 * group, n) for n in (0, 1)]
            + [column_spec(1)],
            scratch_shapes=[
                pltpu.VMEM((2, SHARDS, ROWS, HEAD_DIM), BF16),
                pltpu.VMEM((2, SHARDS, HEAD_DIM, ROWS), BF16),
                pltpu.VMEM((2, group, HEAD_DIM), BF16),
                pltpu.VMEM((2, HEAD_DIM, group), BF16),
                pltpu.VMEM((group, HEAD_DIM), BF16),
                pltpu.VMEM((2 * SHARDS, ROWS, ROWS), F32),
                pltpu.VMEM((8, ROWS), F32),
                pltpu.VMEM((2, SHARDS, ROWS, HEAD_DIM), BF16),
                pltpu.VMEM((2, group + 2 * ROWS, group), F32),
                pltpu.VMEM((2, group + 2 * ROWS, group), BF16),
                pltpu.VMEM((2, SHARDS, ROWS, HEAD_DIM), F32),
            ],
        ),
        out_shape=(
            *(jax.ShapeDtypeStruct(shape, BF16) for shape in outs),
            jax.ShapeDtypeStruct((1, part), F32),
        ),
        compiler_params=pltpu.CompilerParams(
            dimension_semantics=("arbitrary",), vmem_limit_bytes=VMEM_BYTES
        ),
        cost_estimate=pl.CostEstimate(
            flops=heads * 12 * group * (group + 2 * ROWS) * HEAD_DIM,
            bytes_accessed=heads * 14 * group * HEAD_DIM * 2,
            transcendentals=heads * group * (group + 2 * ROWS),
        ),
        name="attend",
    )(scalars, *own, *prior_kv, gain_row)


def finish_kernel(gain, own, back_0, back_1, rest_2, *outs):
    outs[2][2 * ROWS :] = rest_2[...]
    for back, (columns, here) in zip((back_0, back_1), place_columns(0, own.shape[1])):
        gain_row = gain[:, columns]
        for s, out in enumerate(outs):
            rows = pl.ds(2 * s * ROWS, ROWS)
            total = own[rows, here].astype(F32) + back[rows].astype(F32)
            out[0:ROWS, here] = (total * gain_row).astype(BF16)
            rows = pl.ds((2 * s + 1) * ROWS, ROWS)
            total = own[rows, here].astype(F32) + back[rows].astype(F32)
            out[ROWS : 2 * ROWS, here] = total.astype(BF16)


def finish(own, backs, rest_2, gain_row):
    width = own.shape[1]
    return pl.pallas_call(
        finish_kernel,
        in_specs=[vmem_spec()] * 5,
        out_specs=(vmem_spec(),) * SHARDS,
        out_shape=tuple(
            jax.ShapeDtypeStruct(((4 if s == 2 else 2) * ROWS, width), BF16)
            for s in range(SHARDS)
        ),
        cost_estimate=pl.CostEstimate(
            flops=16 * ROWS * width, bytes_accessed=48 * ROWS * width, transcendentals=0
        ),
        compiler_params=pltpu.CompilerParams(vmem_limit_bytes=VMEM_BYTES),
        name="finish",
    )(gain_row, own, *backs, rest_2)


def shifted_halves(first, second, steps):
    outer, inner = lax.axis_size("outer"), lax.axis_size("inner")
    straight, turned = [], []
    for o in range(outer):
        target = (o + steps) % outer
        turn = o // (outer // 2) - target // (outer // 2)
        for i in range(inner):
            straight.append((o * inner + i, target * inner + i))
            turned.append((o * inner + i, target * inner + (i + turn) % inner))
    axes = ("outer", "inner")
    return (
        [lax.ppermute(x, axes, straight) for x in first],
        [lax.ppermute(x, axes, turned) for x in second],
    )


def gathered(term):
    for step in (1, 2):
        pairs = [(source, source ^ step) for source in range(lax.axis_size("inner"))]
        term = jnp.concatenate([term, lax.ppermute(term, "inner", pairs)])
    return term


STEPS = (("dp", 1), ("dp", 2), ("outer", 2), ("outer", 4), ("outer", 1))


def sum_by_steps(steps, term):
    for axis, step in steps:
        pairs = [(source, source ^ step) for source in range(lax.axis_size(axis))]
        term = term + lax.ppermute(term, axis, pairs)
    half = term.shape[1] // 2
    (first,), (second,) = shifted_halves(
        (term[:, :half],), (term[:, half:],), lax.axis_size("outer") // 2
    )
    return gathered(term + jnp.concatenate([first, second], axis=1))


def body(queries, keys, values, out_grad, gain, block_order, start):
    inner = lax.axis_index("inner").astype(jnp.int32)
    turn = lax.axis_index("outer") // (lax.axis_size("outer") // 2)
    scalars = jnp.stack([inner, start[0], lax.rem(inner + turn, SHARDS)])
    gain_row = gain[None]

    own = pack(block_order, queries, keys, values, out_grad)
    own = [own[0]] + [permuted(own[k], "inner", k) for k in range(1, SHARDS)]
    early, late = join([own[0], own[1], own[3]]), join([own[2]])
    prior_0, prior_1 = shifted_halves((early[0], late[0]), (early[1], late[1]), 1)
    *ad, own_part, prior_part_0, prior_part_1, term = attend(
        scalars, own, [*prior_0, *prior_1], gain_row
    )

    (back_0,), (back_1,) = shifted_halves((prior_part_0,), (prior_part_1,), -1)
    ad_1, ad_3 = permuted(ad[1], "inner", -1), permuted(ad[3], "inner", -3)
    back_0, ad_1, ad_3 = lax.optimization_barrier((back_0, ad_1, ad_3))
    parts = finish(own_part, (back_0, back_1), ad[2], gain_row)
    term, ad_0, _ = lax.optimization_barrier((term, ad[0], parts[0]))
    parts = [parts[0]] + [permuted(parts[k], "inner", -k) for k in range(1, SHARDS)]
    attended, query_grad = unpack_early((ad_0, ad_1, ad_3))
    term, attended = lax.optimization_barrier((term, attended))
    terms = lax.cond(
        start[0] >= 0,
        functools.partial(sum_by_steps, STEPS),
        functools.partial(sum_by_steps, STEPS[::-1]),
        term,
    )
    token_count = (
        ROWS * lax.axis_size("inner") * lax.axis_size("outer") * lax.axis_size("dp")
    )
    attended, query_grad, key_grad, value_grad, gain_grad = unpack(
        parts, terms, attended, query_grad, 1.0 / math.sqrt(token_count)
    )
    return attended, query_grad, key_grad, value_grad, gain_grad.reshape(-1)


def solution(mesh):
    rows = P("dp", ("outer", "inner"), None)
    in_specs = (rows, rows, rows, rows, P(), P(("outer", "inner")), P())
    out_specs = (rows, rows, rows, rows, P())
    return jax.shard_map(body, mesh=mesh, in_specs=in_specs, out_specs=out_specs, check_vma=False)
```

```python
import functools
import math

import jax
import jax.numpy as jnp
from jax import lax
from jax.experimental import pallas as pl
from jax.experimental.pallas import tpu as pltpu
from jax.sharding import PartitionSpec as P

HEAD_DIM = 128
ROWS = 128
SHARDS = 4
EXTRA_ROWS = 16
KV_ROWS = 2 * ROWS + EXTRA_ROWS
VMEM_BYTES = 56 * 1024 * 1024
F32 = jnp.float32
BF16 = jnp.bfloat16


def permuted(value, axis, steps):
    count = lax.axis_size(axis)
    pairs = [(source, (source + steps) % count) for source in range(count)]
    return lax.ppermute(value, axis, pairs)


def vmem_spec():
    return pl.BlockSpec(memory_space=pltpu.VMEM)


def smem_spec():
    return pl.BlockSpec(memory_space=pltpu.SMEM)


def any_spec():
    return pl.BlockSpec(memory_space=pl.ANY)


def place_columns(k, width):
    return block_columns(lax.rem(lax.axis_index("inner") + k, SHARDS), width)


def block_columns(place, width):
    half = width // 2
    turn = lax.axis_index("outer") // (lax.axis_size("outer") // 2)
    first = place * width
    second = lax.rem(place + turn, SHARDS) * width + half
    return (
        (pl.ds(pl.multiple_of(first, half), half), slice(0, half)),
        (pl.ds(pl.multiple_of(second, half), half), slice(half, width)),
    )


def put_kv(out, k, order, keys, values):
    width = out.shape[1]
    for columns, here in place_columns(k, width):
        out[0:ROWS, here] = keys[0, :, columns]
        out[ROWS : 2 * ROWS, here] = values[0, :, columns]
    rows = lax.broadcasted_iota(jnp.int32, (EXTRA_ROWS, width), 0)
    numbers = jnp.where(rows < EXTRA_ROWS // 2, order[0], order[1])
    out[2 * ROWS : KV_ROWS] = numbers.astype(F32).astype(BF16)


def put_qd(out, first, k, queries, grads):
    for columns, here in place_columns(k, out.shape[1]):
        out[first : first + ROWS, here] = queries[0, :, columns]
        out[first + ROWS : first + 2 * ROWS, here] = grads[0, :, columns]


def join_kernel(*refs):
    parts, outs = refs[:-2], refs[-2:]
    half = parts[0].shape[1] // 2
    for n, out in enumerate(outs):
        for s, part in enumerate(parts):
            rows = slice(s * KV_ROWS, (s + 1) * KV_ROWS)
            out[rows] = part[0:KV_ROWS, n * half : (n + 1) * half]


def join(parts):
    out = jax.ShapeDtypeStruct((len(parts) * KV_ROWS, parts[0].shape[1] // 2), BF16)
    return pl.pallas_call(
        join_kernel,
        out_shape=(out, out),
        in_specs=[vmem_spec()] * len(parts),
        out_specs=(vmem_spec(),) * 2,
        compiler_params=pltpu.CompilerParams(vmem_limit_bytes=VMEM_BYTES),
        name="join",
    )(*parts)


def pack_kernel(order, queries, keys, values, grads, *outs):
    for k, out in enumerate(outs):
        put_kv(out, k, order, keys, values)
        put_qd(out, KV_ROWS, k, queries, grads)


def pack(order, queries, keys, values, grads):
    out = jax.ShapeDtypeStruct((KV_ROWS + 2 * ROWS, keys.shape[2] // SHARDS), BF16)
    return pl.pallas_call(
        pack_kernel,
        out_shape=(out,) * SHARDS,
        in_specs=[smem_spec()] + [vmem_spec()] * 4,
        out_specs=(vmem_spec(),) * SHARDS,
        compiler_params=pltpu.CompilerParams(vmem_limit_bytes=VMEM_BYTES),
        name="pack",
    )(order, queries, keys, values, grads)


def copies_out(k, part, first, outs, sems):
    copies = []
    for h, (columns, here) in enumerate(place_columns(k, part.shape[1])):
        for n, out in enumerate(outs):
            source = part.at[first + n * ROWS : first + (n + 1) * ROWS, here]
            sem = sems.at[2 * h + n]
            copies.append(pltpu.make_async_copy(source, out.at[0, :, columns], sem))
    return copies


def unpack_kernel(gain_scale, *refs):
    parts, terms = refs[:SHARDS], refs[SHARDS]
    part_0, part_1, part_3 = refs[SHARDS + 1 : SHARDS + 4]
    attended, query_grad, key_grad, value_grad, gain_grad, sems = refs[SHARDS + 4 :]
    copies = []
    for n, (k, part) in enumerate(((0, part_0), (1, part_1), (3, part_3))):
        copies += copies_out(k, part, 0, (attended, query_grad), sems.at[SHARDS + 1 + n])
    for k, part in enumerate(parts):
        copies += copies_out(k, part, 0, (key_grad, value_grad), sems.at[k])
    copies += copies_out(2, parts[2], 2 * ROWS, (attended, query_grad), sems.at[SHARDS])
    for copy in copies:
        copy.start()
    for n in range(SHARDS):
        for columns, here in block_columns(lax.axis_index("inner") ^ n, terms.shape[1]):
            gain_grad[:, columns] = terms[n : n + 1, here] * gain_scale
    for copy in copies:
        copy.wait()


def unpack(parts, terms, early, gain_scale):
    channels = terms.shape[1] * SHARDS
    out = jax.ShapeDtypeStruct((1, ROWS, channels), BF16)
    return pl.pallas_call(
        functools.partial(unpack_kernel, gain_scale),
        out_shape=(out,) * 4 + (jax.ShapeDtypeStruct((1, channels), F32),),
        in_specs=[vmem_spec()] * (2 * SHARDS),
        out_specs=(any_spec(),) * 4 + (vmem_spec(),),
        scratch_shapes=[pltpu.SemaphoreType.DMA((2 * SHARDS, 4))],
        compiler_params=pltpu.CompilerParams(vmem_limit_bytes=VMEM_BYTES),
        name="unpack",
    )(*parts, terms, *early)


def dot_nn(a, b):
    return lax.dot_general(a, b, (((1,), (0,)), ((), ())), preferred_element_type=F32)


def dot_nt(a, b):
    return lax.dot_general(a, b, (((1,), (1,)), ((), ())), preferred_element_type=F32)


def attend_kernel(scalars, *refs):
    own_kv = refs[0:4]
    qd = [ref.at[KV_ROWS:] for ref in own_kv]
    halves = (refs[4:6], refs[6:8])
    prior_place = ((0, 0), (0, KV_ROWS), (1, 0), (0, 2 * KV_ROWS))
    gain = refs[8]
    ad_out = refs[9:13]
    own_out = refs[13]
    prior_outs, gain_out = refs[14:16], refs[16]
    own, own_t, prior, prior_t, raw_prior, kpos, qpos, q_all, s_all, w_all, step_part = refs[17:]
    head, heads = pl.program_id(0), pl.num_programs(0)
    start = scalars[1]
    group = SHARDS * ROWS
    score_scale = HEAD_DIM ** (-0.5)
    exponent_scale = score_scale * math.log2(math.e)
    half = ROWS // 2
    key_at, value_at = 0, 1
    query_at, grad_at = 0, 1
    weight_at, score_at = 0, 1

    in_first = head < heads // 2
    lane = lax.broadcasted_iota(jnp.int32, (1, ROWS), 1)
    lanes = jnp.where(lane < half, lane, lane - half).astype(F32)
    row = lax.broadcasted_iota(jnp.int32, (half, ROWS), 0).astype(F32)
    own_numbers = [ref[2 * ROWS : KV_ROWS] for ref in own_kv]
    prior_numbers = [
        jnp.where(in_first, *(parts[at][first + 2 * ROWS : first + KV_ROWS] for parts in halves))
        for at, first in prior_place
    ]
    for s, numbers in enumerate(own_numbers + prior_numbers):
        numbers = numbers.astype(F32)
        first = numbers[0:1] * half
        second = numbers[EXTRA_ROWS // 2 : EXTRA_ROWS // 2 + 1] * half
        kpos[s, 0:half] = row + first
        kpos[s, half:ROWS] = row + second
        if s < SHARDS:
            qpos[s : s + 1] = jnp.where(lane < half, first, second) + lanes

    gain_row = gain[...]
    for s in range(SHARDS):
        rows = slice(s * ROWS, (s + 1) * ROWS)
        for n in (key_at, value_at):
            part = own_kv[s][n * ROWS : (n + 1) * ROWS]
            if n == key_at:
                part = (part.astype(F32) * gain_row).astype(BF16)
            own[n, s] = part
            own_t[n, s] = part.T
        q_all[query_at, s] = qd[s][0:ROWS]
        q_all[grad_at, s] = qd[s][ROWS : 2 * ROWS]
    for s, (part_at, first) in enumerate(prior_place):
        rows = slice(s * ROWS, (s + 1) * ROWS)
        raw, value = (
            jnp.where(in_first, *(half[part_at][at : at + ROWS] for half in halves))
            for at in (first, first + ROWS)
        )
        raw_prior[rows] = raw
        key = (raw.astype(F32) * gain_row).astype(BF16)
        for n, part in ((key_at, key), (value_at, value)):
            prior[n, rows] = part
            prior_t[n, :, rows] = part.T

    steps = [lax.rem(start + a, SHARDS) for a in range(SHARDS)]
    columns = [slice(a * ROWS, (a + 1) * ROWS) for a in range(SHARDS)]
    for n in (0, 1):
        s_all[n, 2 * ROWS :] = dot_nt(prior[n], q_all[n].reshape(group, HEAD_DIM))
    for n in (0, 1):
        for a in range(SHARDS):
            s_all[n, 0:ROWS, columns[a]] = dot_nt(own[n, a], q_all[n, a])
            s_all[n, ROWS : 2 * ROWS, columns[a]] = dot_nt(own[n, steps[a]], q_all[n, a])

    for a in range(SHARDS):
        query_pos = qpos[a : a + 1]
        parts = []
        for first, positions in (
            (0, kpos[a]),
            (ROWS, kpos[steps[a]]),
            (2 * ROWS, kpos[SHARDS:].reshape(group, ROWS)),
        ):
            raw = s_all[0, first : first + positions.shape[0], columns[a]] * exponent_scale
            parts.append(jnp.where(positions <= query_pos, raw, -jnp.inf))
        scores = jnp.concatenate(parts, axis=0)
        exps = jnp.exp2(scores - jnp.max(scores, axis=0, keepdims=True))
        weights = exps * (1.0 / jnp.sum(exps, axis=0, keepdims=True))
        s_all[0, :, columns[a]] = weights
        w_all[weight_at, :, columns[a]] = weights.astype(BF16)

    def times_weights(n, which):
        total = dot_nn(prior_t[n], w_all[which, 2 * ROWS :])
        return [
            total[:, columns[a]]
            + dot_nn(own_t[n, a], w_all[which, 0:ROWS, columns[a]])
            + dot_nn(own_t[n, steps[a]], w_all[which, ROWS : 2 * ROWS, columns[a]])
            for a in range(SHARDS)
        ]

    attended_t = times_weights(value_at, weight_at)
    for a in range(SHARDS):
        ad_out[a][0:ROWS] = attended_t[a].T.astype(BF16)
        rounded = attended_t[a].astype(BF16).astype(F32)
        grad_t = q_all[grad_at, a].astype(F32).T
        row_dot = jnp.sum(grad_t * rounded, axis=0, keepdims=True)
        weights = s_all[0, :, columns[a]]
        score_grad = weights * (s_all[1, :, columns[a]] - row_dot)
        w_all[score_at, :, columns[a]] = score_grad.astype(BF16)
    query_grad_t = times_weights(key_at, score_at)
    for a in range(SHARDS):
        ad_out[a][ROWS : 2 * ROWS] = (query_grad_t[a] * score_scale).T.astype(BF16)

    gain_sum = jnp.zeros((1, HEAD_DIM), F32)
    queries, grads = (q_all[n].reshape(group, HEAD_DIM) for n in (0, 1))
    prior_key = dot_nn(w_all[score_at, 2 * ROWS :], queries) * score_scale
    prior_value = dot_nn(w_all[weight_at, 2 * ROWS :], grads)
    gain_sum += jnp.sum(prior_key * raw_prior[...].astype(F32), axis=0, keepdims=True)
    for half_at, out in enumerate(prior_outs):

        @pl.when(head // (heads // 2) == half_at)
        def _(out=out):
            for s in range(SHARDS):
                rows = slice(s * ROWS, (s + 1) * ROWS)
                out[2 * s * ROWS : (2 * s + 1) * ROWS] = prior_key[rows].astype(BF16)
                out[(2 * s + 1) * ROWS : (2 * s + 2) * ROWS] = prior_value[rows].astype(BF16)

    for n in (0, 1):
        which, source = ((score_at, query_at), (weight_at, grad_at))[n]
        for a in range(SHARDS):
            step_part[n, steps[a]] = dot_nn(w_all[which, ROWS : 2 * ROWS, columns[a]], q_all[source, a])
    for s in range(SHARDS):
        key_part = dot_nn(w_all[score_at, 0:ROWS, columns[s]], q_all[query_at, s])
        key_part = (key_part + step_part[0, s]) * score_scale
        value_part = dot_nn(w_all[weight_at, 0:ROWS, columns[s]], q_all[grad_at, s])
        value_part = value_part + step_part[1, s]
        own_out[2 * s * ROWS : (2 * s + 1) * ROWS] = key_part.astype(BF16)
        own_out[(2 * s + 1) * ROWS : (2 * s + 2) * ROWS] = value_part.astype(BF16)
        raw = own_kv[s][0:ROWS].astype(F32)
        gain_sum += jnp.sum(key_part * raw, axis=0, keepdims=True)
    gain_out[...] = jnp.broadcast_to(gain_sum, gain_out.shape)


def attend(scalars, own, prior_kv, gain_row):
    part = own[0].shape[1]
    heads = part // HEAD_DIM
    group = SHARDS * ROWS

    def column_spec(rows):
        return pl.BlockSpec((rows, HEAD_DIM), lambda h, sc: (0, h))

    half = heads // 2

    def half_spec(rows, n):
        if n == 0:
            return pl.BlockSpec((rows, HEAD_DIM), lambda h, sc: (0, jnp.minimum(h, half - 1)))
        return pl.BlockSpec((rows, HEAD_DIM), lambda h, sc: (0, jnp.maximum(h - half, 0)))

    gain_spec = pl.BlockSpec(
        (1, HEAD_DIM), lambda h, sc: (0, jnp.where(h < half, sc[0], sc[2]) * heads + h)
    )
    outs = [(2 * ROWS, part)] * 4 + [(2 * group, part)] + [(2 * group, part // 2)] * 2
    return pl.pallas_call(
        attend_kernel,
        grid_spec=pltpu.PrefetchScalarGridSpec(
            num_scalar_prefetch=1,
            grid=(heads,),
            in_specs=[column_spec(x.shape[0]) for x in own]
            + [half_spec(x.shape[0], n // 2) for n, x in enumerate(prior_kv)]
            + [gain_spec],
            out_specs=[column_spec(rows) for rows, _ in outs[:5]]
            + [half_spec(2 * group, n) for n in (0, 1)]
            + [column_spec(1)],
            scratch_shapes=[
                pltpu.VMEM((2, SHARDS, ROWS, HEAD_DIM), BF16),
                pltpu.VMEM((2, SHARDS, HEAD_DIM, ROWS), BF16),
                pltpu.VMEM((2, group, HEAD_DIM), BF16),
                pltpu.VMEM((2, HEAD_DIM, group), BF16),
                pltpu.VMEM((group, HEAD_DIM), BF16),
                pltpu.VMEM((2 * SHARDS, ROWS, ROWS), F32),
                pltpu.VMEM((8, ROWS), F32),
                pltpu.VMEM((2, SHARDS, ROWS, HEAD_DIM), BF16),
                pltpu.VMEM((2, group + 2 * ROWS, group), F32),
                pltpu.VMEM((2, group + 2 * ROWS, group), BF16),
                pltpu.VMEM((2, SHARDS, ROWS, HEAD_DIM), F32),
            ],
        ),
        out_shape=(
            *(jax.ShapeDtypeStruct(shape, BF16) for shape in outs),
            jax.ShapeDtypeStruct((1, part), F32),
        ),
        compiler_params=pltpu.CompilerParams(
            dimension_semantics=("arbitrary",), vmem_limit_bytes=VMEM_BYTES
        ),
        cost_estimate=pl.CostEstimate(
            flops=heads * 12 * group * (group + 2 * ROWS) * HEAD_DIM,
            bytes_accessed=heads * 14 * group * HEAD_DIM * 2,
            transcendentals=heads * group * (group + 2 * ROWS),
        ),
        name="attend",
    )(scalars, *own, *prior_kv, gain_row)


def finish_kernel(gain, own, back_0, back_1, rest_2, *outs):
    outs[2][2 * ROWS :] = rest_2[...]
    for back, (columns, here) in zip((back_0, back_1), place_columns(0, own.shape[1])):
        gain_row = gain[:, columns]
        for s, out in enumerate(outs):
            rows = pl.ds(2 * s * ROWS, ROWS)
            total = own[rows, here].astype(F32) + back[rows].astype(F32)
            out[0:ROWS, here] = (total * gain_row).astype(BF16)
            rows = pl.ds((2 * s + 1) * ROWS, ROWS)
            total = own[rows, here].astype(F32) + back[rows].astype(F32)
            out[ROWS : 2 * ROWS, here] = total.astype(BF16)


def finish(own, backs, rest_2, gain_row):
    width = own.shape[1]
    return pl.pallas_call(
        finish_kernel,
        in_specs=[vmem_spec()] * 5,
        out_specs=(vmem_spec(),) * SHARDS,
        out_shape=tuple(
            jax.ShapeDtypeStruct(((4 if s == 2 else 2) * ROWS, width), BF16)
            for s in range(SHARDS)
        ),
        cost_estimate=pl.CostEstimate(
            flops=16 * ROWS * width, bytes_accessed=48 * ROWS * width, transcendentals=0
        ),
        compiler_params=pltpu.CompilerParams(vmem_limit_bytes=VMEM_BYTES),
        name="finish",
    )(gain_row, own, *backs, rest_2)


def shifted_halves(first, second, steps):
    outer, inner = lax.axis_size("outer"), lax.axis_size("inner")
    straight, turned = [], []
    for o in range(outer):
        target = (o + steps) % outer
        turn = o // (outer // 2) - target // (outer // 2)
        for i in range(inner):
            straight.append((o * inner + i, target * inner + i))
            turned.append((o * inner + i, target * inner + (i + turn) % inner))
    axes = ("outer", "inner")
    return (
        [lax.ppermute(x, axes, straight) for x in first],
        [lax.ppermute(x, axes, turned) for x in second],
    )


def gathered(term):
    for step in (1, 2):
        pairs = [(source, source ^ step) for source in range(lax.axis_size("inner"))]
        term = jnp.concatenate([term, lax.ppermute(term, "inner", pairs)])
    return term


STEPS = (("dp", 1), ("dp", 2), ("outer", 2), ("outer", 4), ("outer", 1))


def sum_by_steps(steps, term):
    for axis, step in steps:
        pairs = [(source, source ^ step) for source in range(lax.axis_size(axis))]
        term = term + lax.ppermute(term, axis, pairs)
    half = term.shape[1] // 2
    (first,), (second,) = shifted_halves(
        (term[:, :half],), (term[:, half:],), lax.axis_size("outer") // 2
    )
    return gathered(term + jnp.concatenate([first, second], axis=1))


def body(queries, keys, values, out_grad, gain, block_order, start):
    inner = lax.axis_index("inner").astype(jnp.int32)
    turn = lax.axis_index("outer") // (lax.axis_size("outer") // 2)
    scalars = jnp.stack([inner, start[0], lax.rem(inner + turn, SHARDS)])
    gain_row = gain[None]

    own = pack(block_order, queries, keys, values, out_grad)
    own = [own[0]] + [permuted(own[k], "inner", k) for k in range(1, SHARDS)]
    early, late = join([own[0], own[1], own[3]]), join([own[2]])
    prior_0, prior_1 = shifted_halves((early[0], late[0]), (early[1], late[1]), 1)
    *ad, own_part, prior_part_0, prior_part_1, term = attend(
        scalars, own, [*prior_0, *prior_1], gain_row
    )

    (back_0,), (back_1,) = shifted_halves((prior_part_0,), (prior_part_1,), -1)
    ad_1, ad_3 = permuted(ad[1], "inner", -1), permuted(ad[3], "inner", -3)
    back_0, ad_1, ad_3 = lax.optimization_barrier((back_0, ad_1, ad_3))
    parts = finish(own_part, (back_0, back_1), ad[2], gain_row)
    term, ad_0, _ = lax.optimization_barrier((term, ad[0], parts[0]))
    parts = [parts[0]] + [permuted(parts[k], "inner", -k) for k in range(1, SHARDS)]
    terms = lax.cond(
        start[0] >= 0,
        functools.partial(sum_by_steps, STEPS),
        functools.partial(sum_by_steps, STEPS[::-1]),
        term,
    )
    token_count = (
        ROWS * lax.axis_size("inner") * lax.axis_size("outer") * lax.axis_size("dp")
    )
    attended, query_grad, key_grad, value_grad, gain_grad = unpack(
        parts, terms, (ad_0, ad_1, ad_3), 1.0 / math.sqrt(token_count)
    )
    return attended, query_grad, key_grad, value_grad, gain_grad.reshape(-1)


def solution(mesh):
    rows = P("dp", ("outer", "inner"), None)
    in_specs = (rows, rows, rows, rows, P(), P(("outer", "inner")), P())
    out_specs = (rows, rows, rows, rows, P())
    return jax.shard_map(body, mesh=mesh, in_specs=in_specs, out_specs=out_specs, check_vma=False)
```
